128 devices in a mesh: row: 8 (over x, core), col: 8 (over y_hi, z), band: 2 (over y_lo).
Axes of the slice: x: 4, y: 4 (y_hi: 2, y_lo: 2; y = y_hi * 2 + y_lo), z: 4, core: 2. Of those that a mesh axis runs over, the one named last changes fastest.
Arguments:
- pair_density: float32 [2048, 16384], P('band', ('row', 'col')), may hold values from -1 to 1
- pair_list: int32 [2048], P('band'), may hold values from 0 to 2047, each once
- valence_energy: float32 [4], replicated, may hold values from -8 to -0.5
- conduction_energy: float32 [512], replicated, may hold values from 0.5 to 12
- coulomb: float32 [16384], P(('row', 'band')), may hold values from 0.5 to 4
Outputs:
- factored: float32 [16384, 16384], P(('row', 'band'), 'col')
The draws below stay inside these ranges and needn't reach their ends.
Inputs may be any that keep to these rules, and one draw needn't show every extreme that they name: `pair_list`: every value of 0 to 2047 appears exactly once.
All inputs are finite; a program needn't handle non-finite values.
Results may differ from the reference program's by a relative error of at most 0.0003.
Values sent between devices are 32-bit elements; how exact they have to be, the bound alone decides.
No kernel may reach another device: no remote copies, remote signals or barrier semaphores. Data moves between devices by JAX's collectives and lax.ppermute only.
A program may use at most 192 MiB of HBM per device.

```python
import math
import jax
import jax.numpy as jnp
from jax import lax

NG = 16384
NV = 4
NC = 512
PANEL = 512
PAIRS = 2048


def draw_pair_density(key, part):
    key = jax.random.fold_in(key, 11)
    noise_key, share_key, shape_key = jax.random.split(key, 3)
    shared_rank = 24
    randoms = jax.random.normal(noise_key, (PAIRS, NG), jnp.float32)
    spread = 1.5
    shares = jax.random.normal(share_key, (PAIRS, shared_rank), jnp.float32)
    shapes = jax.random.normal(shape_key, (shared_rank, NG), jnp.float32) * (spread / math.sqrt(shared_rank))
    summed = randoms
    for column in range(shared_rank):
        summed = summed + shares[:, column:column + 1] * shapes[column:column + 1, :]
    return jnp.clip(summed * (1.0 / math.sqrt(PAIRS)), -1.0, 1.0)


def steps_of(rng, shape, pieces, low, largest):
    loudness = 1.0
    for position, blocks in pieces:
        steps = jax.random.uniform(jax.random.fold_in(jax.random.fold_in(rng, 6), position), (blocks,), jnp.float32, low / len(pieces), largest / len(pieces))
        loudness = loudness * jnp.repeat(jnp.exp(steps), shape[position] // blocks).reshape((-1,) + (1,) * (len(shape) - 1 - position))
    return loudness


def setup_inputs(seed: int = 0) -> dict:
    streams_of = jax.random.split(jax.random.key(seed), 6)
    pair_density = draw_pair_density(jax.random.fold_in(streams_of[5], 71), 0)
    pair_list = jax.random.permutation(streams_of[1], PAIRS).astype(jnp.int32)
    valence_energy = jnp.clip(jax.random.uniform(streams_of[2], (NV,), jnp.float32, -8.0, -0.5), -8.0, -0.5)
    conduction_energy = jnp.clip(jax.random.uniform(streams_of[3], (NC,), jnp.float32, 0.5, 12.0), 0.5, 12.0)
    coulomb = jnp.clip(jnp.exp(math.log(4.0) - 2.0794415 * jax.random.uniform(streams_of[4], (NG,), jnp.float32) ** steps_of(streams_of[4], (NG,), ((0, 16),), -0.2, 0.2)), 0.5, 4.0)
    return dict(pair_density=pair_density, pair_list=pair_list, valence_energy=valence_energy, conduction_energy=conduction_energy, coulomb=coulomb)


def factor_leaf(matrix):
    extent = matrix.shape[0]
    indices = jnp.arange(extent, dtype=jnp.int32)

    def eliminate(pivot, current):
        pivot_row = lax.dynamic_index_in_dim(current, pivot, 0, keepdims=False)
        pivot_col = lax.dynamic_index_in_dim(current, pivot, 1, keepdims=False)
        below = indices > pivot
        factors = jnp.where(below, pivot_col / pivot_row[pivot], 0.0)
        current = current - factors[:, None] * jnp.where(below, pivot_row, 0.0)[None, :]
        return jnp.where((indices[None, :] == pivot) & below[:, None], factors[:, None], current)
    return lax.fori_loop(0, extent, eliminate, matrix)

def factor_block(matrix):
    extent = matrix.shape[0]
    if extent <= 16:
        return factor_leaf(matrix)
    middle = extent // 2
    upper_left = factor_block(matrix[:middle, :middle])
    lower_unit = jnp.tril(upper_left, -1) + jnp.eye(middle, dtype=matrix.dtype)
    upper_tri = jnp.triu(upper_left)
    right_rows = jax.scipy.linalg.solve_triangular(lower_unit, matrix[:middle, middle:], lower=True, unit_diagonal=True)
    left_rows = jax.scipy.linalg.solve_triangular(upper_tri.T, matrix[middle:, :middle].T, lower=True).T
    schur = matrix[middle:, middle:] - jnp.dot(left_rows, right_rows, precision=lax.Precision.HIGHEST)
    lower_right = factor_block(schur)
    return jnp.concatenate([jnp.concatenate([upper_left, right_rows], 1), jnp.concatenate([left_rows, lower_right], 1)], 0)

def reference(pair_density, pair_list, valence_energy, conduction_energy, coulomb):
    valence_index = pair_list // NC
    conduction_index = pair_list % NC
    gaps = conduction_energy[conduction_index] - valence_energy[valence_index]
    weights = 4.0 / gaps
    scaled = pair_density * weights[:, None]
    chi_sum = lax.dot_general(scaled.astype(jnp.float32), pair_density.astype(jnp.float32), (((0,), (0,)), ((), ())), precision=lax.Precision.HIGHEST, preferred_element_type=jnp.float32)
    dielectric = jnp.eye(NG, dtype=jnp.float32) + coulomb[:, None] * chi_sum
    diag_factor = factor_block(dielectric[:PANEL, :PANEL])
    lower_unit = jnp.tril(diag_factor, -1) + jnp.eye(PANEL, dtype=jnp.float32)
    upper_tri = jnp.triu(diag_factor)
    upper_factor = jax.scipy.linalg.solve_triangular(lower_unit, dielectric[:PANEL, PANEL:], lower=True, unit_diagonal=True)
    left_factor = jax.scipy.linalg.solve_triangular(upper_tri.T, dielectric[PANEL:, :PANEL].T, lower=True).T
    schur = dielectric[PANEL:, PANEL:] - jnp.dot(left_factor, upper_factor, precision=lax.Precision.HIGHEST)
    top = jnp.concatenate([diag_factor, upper_factor], 1)
    bottom = jnp.concatenate([left_factor, schur], 1)
    return jnp.concatenate([top, bottom], 0)
```

```python
import functools

import jax
import jax.numpy as jnp
from jax import lax
from jax.experimental import pallas as pl
from jax.experimental.pallas import tpu as pltpu
from jax.sharding import Mesh, PartitionSpec as P

PANEL = 512
PAIRS = 2048
HALF = 1024
ROWS = 1024
COLS = 2048
PIECE = 256
BLOCK = 128
GROUP = 8
AXES = ("x", "k", "h", "z", "l")
SIZES = (4, 2, 2, 4, 2)
F32 = jnp.float32
BF16 = jnp.bfloat16
VMEM = pltpu.VMEM
MIB = 2**20


def position(x, k, h, z, l):
    return (((x * 2 + k) * 2 + h) * 4 + z) * 2 + l


def move(value, target):
    pairs = []
    for x in range(4):
        for k in range(2):
            for h in range(2):
                for z in range(4):
                    for l in range(2):
                        to = target(x, k, h, z, l)
                        if to is not None:
                            pairs.append((position(x, k, h, z, l), position(*to)))
    return lax.ppermute(value, AXES, pairs)


def x_ring(step):
    return lambda x, k, h, z, l: ((x + (step if k == 0 else -step)) % 4, k, h, z, l)


def z_ring(step):
    return lambda x, k, h, z, l: (x, k, h, (z + step) % 4, l)


def other_core(x, k, h, z, l):
    return (x, 1 - k, h, z, l)


def other_band(x, k, h, z, l):
    return (x, k, h, z, 1 - l)


def to_column_line(x, k, h, z, l):
    return ((x + 2 * (z & 1) + (z >> 1)) % 4, h, x >> 1, (x & 1) * 2 + k, l)


def rows_first(x, k, h, z, l):
    to = {0: 2, 1: 0, 2: 3, 3: 1}[2 * h + l]
    return (x, k, to >> 1, z, to & 1)


def rows_second(x, k, h, z, l):
    to = {1: 2, 2: 1}.get(2 * h + l)
    return None if to is None else (x, k, to >> 1, z, to & 1)


def spread_panel(piece, x, k, h, z):
    part = move(
        piece[512:], lambda x, k, h, z, l: (0, 1, 0, z, l) if x == k == h == 0 and z < 2 else None
    )
    held = jnp.where(k == 1, part, piece[:512])
    part = move(
        held[256:], lambda x, k, h, z, l: (2, k, 0, z, l) if x == h == 0 and z < 2 else None
    )
    held = jnp.where(x >= 2, part, held[:256])
    part = move(
        held[128:],
        lambda x, k, h, z, l: (x + 1, k, 0, z, l) if x % 2 == 0 and h == 0 and z < 2 else None,
    )
    held = jnp.where(x % 2 == 1, part, held[:128])
    part = move(held, lambda x, k, h, z, l: (x, k, 0, z + 2, l) if h == 0 and z < 2 else None)
    held = jnp.where(z >= 2, part, held)
    part = move(held, lambda x, k, h, z, l: (x, k, 1, z, l) if h == 0 else None)
    held = jnp.where(h == 1, part, held)
    part = move(held, lambda x, k, h, z, l: (x, k, h, z ^ 1, l))
    even = z % 2 == 0
    both = jnp.concatenate([jnp.where(even, held, part), jnp.where(even, part, held)], axis=1)
    return lax.all_gather(both, ("l", "k", "x"), axis=0, tiled=True)


def exact_dot(a, b, dims):
    return lax.dot_general(
        a, b, (dims, ((), ())), precision=lax.Precision.HIGHEST, preferred_element_type=F32
    )


def factor_unit(a):
    n = BLOCK
    row_id = lax.broadcasted_iota(jnp.int32, (n, n), 0)
    col_id = lax.broadcasted_iota(jnp.int32, (n, n), 1)
    inv = jnp.where(row_id == col_id, 1.0, 0.0).astype(F32)
    upper_rows, inverse_rows = [], []
    for first in range(0, n, GROUP):
        m = n - first
        cols = [jnp.broadcast_to(a[:, first + t : first + t + 1], (m, n)) for t in range(GROUP)]
        rows = [a[t : t + 1, :] for t in range(GROUP)]
        irows = [inv[t : t + 1, :] for t in range(GROUP)]
        below = lax.broadcasted_iota(jnp.int32, (m, n), 0) >= GROUP
        for t in range(GROUP):
            recip = 1.0 / cols[t][t : t + 1, :]
            for u in range(t + 1, GROUP):
                factor = cols[t][u : u + 1, :] * recip
                rows[u] = rows[u] - factor * rows[t]
                irows[u] = irows[u] - factor * irows[t]
                cols[u] = cols[u] - cols[t] * factor
            low = jnp.where(below, cols[t], 0.0)
            a = a - low * (rows[t] * recip)
            inv = inv - low * (irows[t] * recip)
            upper_rows.append(rows[t])
            inverse_rows.append(irows[t])
        if m > GROUP:
            a, inv = a[GROUP:, :], inv[GROUP:, :]
    return upper_rows, inverse_rows


def factor_kernel(b_ref, y_ref, inv_ref, dinv_ref, work, iwork):
    n = b_ref.shape[0]
    work[...] = b_ref[...]
    row_id = lax.broadcasted_iota(jnp.int32, (n, n), 0)
    col_id = lax.broadcasted_iota(jnp.int32, (n, n), 1)
    inv_ref[...] = jnp.where(row_id == col_id, 1.0, 0.0).astype(F32)
    br = lax.broadcasted_iota(jnp.int32, (BLOCK, BLOCK), 0)
    bc = lax.broadcasted_iota(jnp.int32, (BLOCK, BLOCK), 1)
    for s in range(0, n, BLOCK):
        e = s + BLOCK
        upper_rows, inverse_rows = factor_unit(work[s:e, s:e])
        for j in range(BLOCK):
            y_ref[s + j : s + j + 1, s:e] = upper_rows[j]
            iwork[j : j + 1, :] = inverse_rows[j]
        yd = jnp.where(bc >= br, y_ref[s:e, s:e], 0.0)
        y_ref[s:e, s:e] = yd
        if s:
            y_ref[s:e, :s] = jnp.zeros((BLOCK, s), F32)
        linv = iwork[...]
        diag = jnp.where(bc == br, yd, 0.0)
        dinv = 1.0 / jnp.sum(diag, axis=1, keepdims=True)
        dinv_ref[:, s:e] = 1.0 / jnp.sum(diag, axis=0, keepdims=True)
        inv_ref[s:e, :e] = exact_dot(linv, inv_ref[s:e, :e], ((1,), (0,)))
        if e < n:
            y = exact_dot(linv, work[s:e, e:], ((1,), (0,)))
            y_ref[s:e, e:] = y
            scaled = y * dinv
            work[e:, e:] = work[e:, e:] - exact_dot(scaled, y, ((0,), (0,)))
            inv_ref[e:, :e] = inv_ref[e:, :e] - exact_dot(scaled, inv_ref[s:e, :e], ((0,), (0,)))


def factor_panel(block):
    n = block.shape[0]
    whole = pl.BlockSpec(memory_space=VMEM)
    return pl.pallas_call(
        factor_kernel,
        out_shape=[
            jax.ShapeDtypeStruct((n, n), F32),
            jax.ShapeDtypeStruct((n, n), F32),
            jax.ShapeDtypeStruct((1, n), F32),
        ],
        in_specs=[whole],
        out_specs=[whole] * 3,
        scratch_shapes=[VMEM((n, n), F32), VMEM((BLOCK, BLOCK), F32)],
        compiler_params=pltpu.CompilerParams(vmem_limit_bytes=32 * MIB),
        cost_estimate=pl.CostEstimate(
            flops=18_000_000_000, bytes_accessed=3 * MIB, transcendentals=0
        ),
        name="factor_panel",
    )(block)


def split(value):
    high = value.astype(BF16)
    return high, (value - high.astype(F32)).astype(BF16)


def dot3(a, b, dims):
    dot = functools.partial(
        lax.dot_general, dimension_numbers=(dims, ((), ())), preferred_element_type=F32
    )
    return dot(a[0], b[0]) + (dot(a[1], b[0]) + dot(a[0], b[1]))


def turn_kernel(place_ref, *refs):
    pieces, (high_ref, low_ref) = refs[:8], refs[8:]
    for s, piece in enumerate(pieces):
        row = pl.multiple_of(place_ref[s, 0] * PIECE, PIECE)
        col = pl.multiple_of(place_ref[s, 1] * HALF, HALF)

        @pl.loop(0, HALF // 256)
        def _(step):
            start = pl.multiple_of(step * 256, 256)
            high, low = split(piece[pl.ds(start, 256), :].T)
            at = pl.multiple_of(col + start, 256)
            high_ref[pl.ds(row, PIECE), pl.ds(at, 256)] = high
            low_ref[pl.ds(row, PIECE), pl.ds(at, 256)] = low


def turn_rows(place, pieces):
    whole = pl.BlockSpec(memory_space=VMEM)
    return pl.pallas_call(
        turn_kernel,
        out_shape=[jax.ShapeDtypeStruct((ROWS, PAIRS), BF16)] * 2,
        in_specs=[pl.BlockSpec(memory_space=pltpu.SMEM)] + [whole] * 8,
        out_specs=[whole] * 2,
        compiler_params=pltpu.CompilerParams(vmem_limit_bytes=40 * MIB),
        cost_estimate=pl.CostEstimate(
            flops=4_000_000_000, bytes_accessed=16 * MIB, transcendentals=0
        ),
        name="turn_rows",
    )(place, *pieces)


def project_kernel(
    where_ref, high_ref, low_ref, g_ref, w_ref, dinv_ref, panel_v_ref, v_ref, diag_ref,
    t_high_ref, t_low_ref, left_ref, g_high, g_low,
):
    step = pl.program_id(0)

    @pl.when(step == 0)
    def _():
        g_high[...], g_low[...] = split(g_ref[...])

    rows = (high_ref[...], low_ref[...])
    g = (g_high[...], g_low[...])
    left = dot3(rows, g, ((1,), (1,))) * dinv_ref[...]
    t = (rows[0].astype(F32) + rows[1].astype(F32)) * w_ref[...]
    t = (t - dot3(split(left), g, ((1,), (0,)))) * v_ref[...]
    t_high_ref[...], t_low_ref[...] = split(t)
    left_ref[...] = left * v_ref[...] / panel_v_ref[...]

    @pl.when((where_ref[0] == 1) & (step < PANEL // 256))
    def _():
        start = pl.multiple_of(step * 256, 256)
        t_high_ref[...], t_low_ref[...] = split(g_ref[pl.ds(start, 256), :] * v_ref[...])
        left_ref[...] = diag_ref[pl.ds(start, 256), :]


def project_rows(first_rows, high, low, g, w, dinv, panel_v, v, diag):
    tile = 256

    def fixed(shape):
        return pl.BlockSpec(shape, lambda i, s: (0, 0))

    def by_row(width):
        return pl.BlockSpec((tile, width), lambda i, s: (i, 0))

    return pl.pallas_call(
        project_kernel,
        out_shape=[
            jax.ShapeDtypeStruct((ROWS, PAIRS), BF16),
            jax.ShapeDtypeStruct((ROWS, PAIRS), BF16),
            jax.ShapeDtypeStruct((ROWS, PANEL), F32),
        ],
        grid_spec=pltpu.PrefetchScalarGridSpec(
            num_scalar_prefetch=1,
            grid=(ROWS // tile,),
            in_specs=[
                by_row(PAIRS), by_row(PAIRS), fixed((PANEL, PAIRS)), fixed((1, PAIRS)),
                fixed((1, PANEL)), fixed((1, PANEL)), by_row(1), fixed((PANEL, PANEL)),
            ],
            out_specs=[by_row(PAIRS), by_row(PAIRS), by_row(PANEL)],
            scratch_shapes=[VMEM((PANEL, PAIRS), BF16)] * 2,
        ),
        compiler_params=pltpu.CompilerParams(vmem_limit_bytes=48 * MIB),
        cost_estimate=pl.CostEstimate(
            flops=13_000_000_000, bytes_accessed=22 * MIB, transcendentals=0
        ),
        name="project_rows",
    )(first_rows, high, low, g, w, dinv, panel_v, v, diag)


def multiply_kernel(last, meta_ref, high_ref, low_ref, *refs):
    pieces, refs = refs[:8], refs[8:]
    step = pl.program_id(0)
    out_ref = refs[-1]
    for s, piece in enumerate(pieces):

        @pl.when(step == s)
        def _():
            product = dot3((high_ref[...], low_ref[...]), split(piece[...]), ((1,), (0,)))
            if not last:
                out_ref[...] = product
            else:
                total_ref = refs[0]
                row_id = lax.broadcasted_iota(jnp.int32, (ROWS, PIECE), 0)
                col_id = lax.broadcasted_iota(jnp.int32, (ROWS, PIECE), 1)
                shift = meta_ref[9] + meta_ref[step] * PIECE - meta_ref[10]
                one = jnp.where(row_id - col_id == shift, 1.0, 0.0)
                out_ref[...] = total_ref[...] + product + one

    if last:
        left_ref = refs[1]
        block = meta_ref[step]

        @pl.when((meta_ref[9] == 0) & (block < PANEL // PIECE))
        def _():
            start = pl.multiple_of(block * PIECE, PIECE)
            out_ref[...] = left_ref[:, pl.ds(start, PIECE)]


def multiply(meta, high, low, pieces, total=None, left=None):
    last = total is not None
    halves = pl.BlockSpec((ROWS, HALF), lambda i, m: (0, m[8]), pipeline_mode=pl.Buffered(1))
    piece = pl.BlockSpec(
        (HALF, PIECE), lambda i, m: (0, 0), pipeline_mode=pl.Buffered(1)
    )
    column = pl.BlockSpec((ROWS, PIECE), lambda i, m: (0, m[i]))
    in_specs = [halves, halves] + [piece] * 8
    operands = [high, low, *pieces]
    aliases = {}
    if last:
        in_specs += [column, pl.BlockSpec((ROWS, PANEL), lambda i, m: (0, 0), pipeline_mode=pl.Buffered(1))]
        operands += [total, left]
        aliases = {11: 0}
    return pl.pallas_call(
        functools.partial(multiply_kernel, last),
        out_shape=jax.ShapeDtypeStruct((ROWS, COLS), F32),
        grid_spec=pltpu.PrefetchScalarGridSpec(
            num_scalar_prefetch=1,
            grid=(8,),
            in_specs=in_specs,
            out_specs=column,
        ),
        input_output_aliases=aliases,
        compiler_params=pltpu.CompilerParams(vmem_limit_bytes=52 * MIB),
        cost_estimate=pl.CostEstimate(
            flops=13_000_000_000, bytes_accessed=24 * MIB, transcendentals=0
        ),
        name="multiply_last" if last else "multiply_first",
    )(meta, *operands)


def table_lookup(positions, table):
    entries = table.shape[0]
    matches = positions[:, None] == jnp.arange(entries, dtype=jnp.int32)[None, :]
    return jnp.sum(jnp.where(matches, table[None, :], 0.0), axis=1)


def pair_weights(entries, valence_energy, conduction_energy):
    cond_count = conduction_energy.shape[0]
    gaps = table_lookup(entries % cond_count, conduction_energy) - table_lookup(
        entries // cond_count, valence_energy
    )
    return 4.0 / gaps


def shards(piece, pair_list, valence_energy, conduction_energy, coulomb):
    x, k, h, z, l = [lax.axis_index(a) for a in AXES]
    panel = spread_panel(piece, x, k, h, z)
    first_rows = (x == 0) & (k == 0) & (l == 0)
    panel_v = lax.psum(jnp.where(first_rows, coulomb[:PANEL], 0.0), ("x", "k", "l"))
    own_w = pair_weights(pair_list, valence_energy, conduction_energy)
    far_w = move(own_w, other_band)
    w = jnp.where(
        l == 0, jnp.concatenate([own_w, far_w]), jnp.concatenate([far_w, own_w])
    )

    own = move(piece, to_column_line)
    far = move(own, other_band)

    def column_pieces(value):
        ahead = move(value, x_ring(1))
        back = move(value, x_ring(-1))
        opposite = move(ahead, x_ring(1))
        held = [value, ahead, back, opposite]
        return held + [move(v, other_core) for v in held]

    first = move(piece, rows_first)
    second = jnp.where(h == l, piece, move(piece, rows_second))
    row_pieces = [first, second]
    first_up, second_up = move(first, z_ring(1)), move(second, z_ring(1))
    first_down, second_down = move(first, z_ring(-1)), move(second, z_ring(-1))
    row_pieces += [first_up, second_up, first_down, second_down]
    row_pieces += [move(first_up, z_ring(1)), move(second_down, z_ring(-1))]
    row_blocks = jnp.stack([z, z, z + 3, z + 3, z + 1, z + 1, z + 2, z + 2]) & 3
    halves = jnp.stack([1 - h, h] * 4)
    turned = turn_rows(jnp.stack([row_blocks, halves], axis=1).astype(jnp.int32), row_pieces)

    own_pieces = column_pieces(own)
    far_pieces = column_pieces(far)

    sign = 1 - 2 * k
    at = jnp.stack([x, x - sign, x + sign, x + 2, x, x + sign, x - sign, x + 2])
    core = jnp.stack([k] * 4 + [1 - k] * 4)
    offset = (at - (2 * h + (z >> 1))) & 3
    blocks = 4 * core + 2 * (offset & 1) + (offset >> 1)
    col_start = (4 * h + z) * COLS
    row_start = ((2 * x + k) * 2 + l) * ROWS
    meta = lambda half: jnp.concatenate(
        [blocks, jnp.stack([half, col_start, row_start])]
    ).astype(jnp.int32)

    with jax.named_scope("panel_block"):
        block = lax.dot_general(
            panel * w[:, None], panel, (((0,), (0,)), ((), ())),
            precision=lax.Precision.HIGHEST, preferred_element_type=F32,
        )
        ids = jnp.arange(PANEL)
        block = block + jnp.where(ids[:, None] == ids[None, :], (1.0 / panel_v)[None, :], 0.0)
    upper, inverse, dinv = factor_panel(block)
    with jax.named_scope("panel_rows"):
        g = lax.dot_general(
            inverse, panel, (((1,), (1,)), ((), ())),
            precision=lax.Precision.HIGHEST, preferred_element_type=F32,
        ) * w[None, :]
    with jax.named_scope("panel_diag"):
        scaled = upper * dinv.reshape(PANEL, 1)
        diag = panel_v[:, None] * jnp.where(
            ids[:, None] <= ids[None, :], upper, scaled.T / panel_v[None, :]
        )
    t_high, t_low, left = project_rows(
        first_rows.astype(jnp.int32)[None], turned[0], turned[1], g, w[None, :], dinv,
        panel_v[None, :], coulomb[:, None], diag,
    )
    total = multiply(meta(l), t_high, t_low, own_pieces)
    return multiply(meta(1 - l), t_high, t_low, far_pieces, total, left)


def solution(mesh):
    fine = Mesh(mesh.devices.reshape(SIZES), AXES)
    in_specs = (P("l", ("x", "k", "h", "z")), P("l"), P(), P(), P(("x", "k", "l")))
    out_specs = P(("x", "k", "l"), ("h", "z"))
    return jax.shard_map(shards, mesh=fine, in_specs=in_specs, out_specs=out_specs, check_vma=False)
```

```python
import functools

import jax
import jax.numpy as jnp
from jax import lax
from jax.experimental import pallas as pl
from jax.experimental.pallas import tpu as pltpu
from jax.sharding import Mesh, PartitionSpec as P

PANEL = 512
PAIRS = 2048
HALF = 1024
ROWS = 1024
COLS = 2048
PIECE = 256
BLOCK = 128
PART = 128
GROUP = 8
AXES = ("x", "k", "h", "z", "l")
SIZES = (4, 2, 2, 4, 2)
F32 = jnp.float32
BF16 = jnp.bfloat16
VMEM = pltpu.VMEM
MIB = 2**20
PARAMS = pltpu.CompilerParams(vmem_limit_bytes=60 * MIB)
IN_HBM = pl.BlockSpec(memory_space=pltpu.HBM)


def cost(us):
    return pl.CostEstimate(flops=us * 10**9, bytes_accessed=us * 10**6, transcendentals=0)


def position(x, k, h, z, l):
    return (((x * 2 + k) * 2 + h) * 4 + z) * 2 + l


def move(value, target):
    pairs = []
    for x in range(4):
        for k in range(2):
            for h in range(2):
                for z in range(4):
                    for l in range(2):
                        to = target(x, k, h, z, l)
                        if to is not None:
                            pairs.append((position(x, k, h, z, l), position(*to)))
    return lax.ppermute(value, AXES, pairs)


def x_ring(step):
    return lambda x, k, h, z, l: ((x + (step if k == 0 else -step)) % 4, k, h, z, l)


def z_ring(step):
    return lambda x, k, h, z, l: (x, k, h, (z + step) % 4, l)


def other_core(x, k, h, z, l):
    return (x, 1 - k, h, z, l)


def other_band(x, k, h, z, l):
    return (x, k, h, z, 1 - l)


def to_column_line(x, k, h, z, l):
    return ((x + 2 * (z & 1) + (z >> 1)) % 4, h, x >> 1, (x & 1) * 2 + k, l)


def along_y(table):
    def target(x, k, h, z, l):
        to = table.get(2 * h + l)
        return None if to is None else (x, k, to >> 1, z, to & 1)

    return target


OUTER = along_y({0: 3, 3: 0, 1: 2, 2: 1})
INNER = along_y({1: 0, 2: 3})
RELAY = along_y({3: 2, 0: 1})


def spread_panel(piece, others, x, k, h, z, l):
    def source(h, z):
        return h == 0 and z < 2

    part = move(
        piece[512:], lambda x, k, h, z, l: (0, 1, 0, z, l) if x == k == 0 and source(h, z) else None
    )
    held = jnp.where(k == 1, part, piece[:512])
    part = move(held[256:], lambda x, k, h, z, l: (2, k, 0, z, l) if x == 0 and source(h, z) else None)
    held = jnp.where(x >= 2, part, held[:256])
    part = move(
        held[128:],
        lambda x, k, h, z, l: (x + 1, k, 0, z, l) if x % 2 == 0 and source(h, z) else None,
    )
    held = jnp.where(x % 2 == 1, part, held[:128])
    held, others = lax.optimization_barrier((held, others))
    part = move(held, lambda x, k, h, z, l: (x, k, h, z, 1 - l) if source(h, z) else None)
    low = l == 0
    held = jnp.stack([jnp.where(low, held, part), jnp.where(low, part, held)])
    part = move(held, lambda x, k, h, z, l: (x, k, 1, z, l) if source(h, z) else None)
    held = jnp.where(h == 1, part, held)
    held, others = lax.optimization_barrier((held, others))
    part = move(held, lambda x, k, h, z, l: (x, k, h, z + 2, l) if z < 2 else None)
    held = jnp.where(z >= 2, part, held)
    part = move(held, lambda x, k, h, z, l: (x, k, h, z ^ 1, l))
    even = z % 2 == 0
    both = jnp.concatenate([jnp.where(even, held, part), jnp.where(even, part, held)], axis=2)
    return both.reshape(2 * PART, PANEL), others


def split3(value):
    high = value.astype(BF16)
    rest = value - high.astype(F32)
    middle = rest.astype(BF16)
    return high, middle, (rest - middle.astype(F32)).astype(BF16)


def exact_dot(a, b, dims):
    a, b = split3(a), split3(b)
    left = jnp.concatenate([a[2], a[0], a[1], a[1], a[0], a[0]], axis=dims[0][0])
    right = jnp.concatenate([b[0], b[2], b[1], b[0], b[1], b[0]], axis=dims[1][0])
    return lax.dot_general(left, right, (dims, ((), ())), preferred_element_type=F32)


def factor_unit(a):
    n = BLOCK
    row_id = lax.broadcasted_iota(jnp.int32, (n, n), 0)
    col_id = lax.broadcasted_iota(jnp.int32, (n, n), 1)
    inv = jnp.where(row_id == col_id, 1.0, 0.0).astype(F32)
    upper_rows, inverse_rows = [], []
    for first in range(0, n, GROUP):
        m = n - first
        cols = [jnp.broadcast_to(a[:, first + t : first + t + 1], (m, n)) for t in range(GROUP)]
        rows = [a[t : t + 1, :] for t in range(GROUP)]
        irows = [inv[t : t + 1, :] for t in range(GROUP)]
        below = lax.broadcasted_iota(jnp.int32, (m, n), 0) >= GROUP
        for t in range(GROUP):
            recip = 1.0 / cols[t][t : t + 1, :]
            for u in range(t + 1, GROUP):
                factor = cols[t][u : u + 1, :] * recip
                rows[u] = rows[u] - factor * rows[t]
                irows[u] = irows[u] - factor * irows[t]
                cols[u] = cols[u] - cols[t] * factor
            low = jnp.where(below, cols[t], 0.0)
            a = a - low * (rows[t] * recip)
            inv = inv - low * (irows[t] * recip)
            upper_rows.append(rows[t])
            inverse_rows.append(irows[t])
        if m > GROUP:
            a, inv = a[GROUP:, :], inv[GROUP:, :]
    return upper_rows, inverse_rows


def split(value):
    high = value.astype(BF16)
    return high, (value - high.astype(F32)).astype(BF16)


def dot3(a, b, dims):
    left = jnp.concatenate([a[0], a[1], a[0]], axis=dims[0][0])
    right = jnp.concatenate([b[0], b[0], b[1]], axis=dims[1][0])
    return lax.dot_general(left, right, (dims, ((), ())), preferred_element_type=F32)


def prepare_kernel(meta_ref, w_ref, *refs):
    parts, refs = refs[:8], refs[8:]
    turned_high, turned_low, block_ref, v_ref, left, right, chunk, sems = refs
    n = PANEL
    copies = [
        pltpu.make_async_copy(part, chunk.at[s], sems.at[s]) for s, part in enumerate(parts)
    ]
    for copy in copies:
        copy.start()
    for s, copy in enumerate(copies):
        copy.wait()
        for half in range(2):
            at = pl.ds(pl.multiple_of(half * HALF + meta_ref[s] * PART, PART), PART)
            rows = chunk[s, half * PART : (half + 1) * PART, :]
            turn = rows.T
            turned_high[:, at], turned_low[:, at] = split(turn)
            left[0, :, at], left[1, :, at] = split(turn * w_ref[:, at])
            right[0, at, :], right[1, at, :] = split(rows)

    v_ref[...] = chunk[meta_ref[8], 2 * PART : 2 * PART + 1, :]
    row_id = lax.broadcasted_iota(jnp.int32, (n, n), 0)
    col_id = lax.broadcasted_iota(jnp.int32, (n, n), 1)
    block_ref[...] = jnp.where(row_id == col_id, 1.0 / v_ref[...], 0.0) + dot3(
        (left[0], left[1]), (right[0], right[1]), ((1,), (0,))
    )


def whole_out(shapes):
    return dict(
        out_shape=[jax.ShapeDtypeStruct(*shape) for shape in shapes],
        out_specs=[pl.BlockSpec(shape, lambda i: (0, 0)) for shape, _ in shapes],
        grid=(1,),
    )


def prepare_panel(meta, w, parts):
    shapes = [
        ((PANEL, PAIRS), BF16), ((PANEL, PAIRS), BF16), ((PANEL, PANEL), F32), ((1, PANEL), F32),
    ]
    return pl.pallas_call(
        prepare_kernel,
        in_specs=[
            pl.BlockSpec(memory_space=pltpu.SMEM), pl.BlockSpec((1, PAIRS), lambda i: (0, 0))
        ] + [IN_HBM] * 8,
        scratch_shapes=[
            VMEM((2, PANEL, PAIRS), BF16), VMEM((2, PAIRS, PANEL), BF16),
            VMEM((8, *parts[0].shape), F32), pltpu.SemaphoreType.DMA((8,)),
        ],
        compiler_params=PARAMS,
        cost_estimate=cost(2),
        name="prepare_panel",
        **whole_out(shapes),
    )(meta, w, *parts)


def panel_kernel(
    first_ref, block_ref, turned_high, turned_low, w_ref, v_ref, g_high, g_low, diag_ref, dinv_ref,
    turned, sems, work, upper, inverse, ywork, iwork,
):
    n = PANEL
    copies = [
        pltpu.make_async_copy(ref, turned.at[i], sems.at[i])
        for i, ref in enumerate((turned_high, turned_low))
    ]
    for copy in copies:
        copy.start()
    row_id = lax.broadcasted_iota(jnp.int32, (n, n), 0)
    col_id = lax.broadcasted_iota(jnp.int32, (n, n), 1)
    one = row_id == col_id
    work[...] = block_ref[...]
    inverse[...] = jnp.where(one, 1.0, 0.0).astype(F32)
    br = lax.broadcasted_iota(jnp.int32, (BLOCK, BLOCK), 0)
    bc = lax.broadcasted_iota(jnp.int32, (BLOCK, BLOCK), 1)
    wide = lax.broadcasted_iota(jnp.int32, (BLOCK, n), 1)

    @pl.loop(0, n // BLOCK)
    def _(step):
        s = pl.multiple_of(step * BLOCK, BLOCK)
        here = pl.ds(s, BLOCK)
        upper_rows, inverse_rows = factor_unit(work[here, here])
        for j in range(BLOCK):
            ywork[j : j + 1, :] = upper_rows[j]
            iwork[j : j + 1, :] = inverse_rows[j]
        unit = jnp.where(bc >= br, ywork[...], 0.0)
        linv = iwork[...]
        diag = jnp.where(bc == br, unit, 0.0)
        dinv = 1.0 / jnp.sum(diag, axis=1, keepdims=True)
        dinv_ref[:, here] = 1.0 / jnp.sum(diag, axis=0, keepdims=True)
        y = jnp.where(wide >= s + BLOCK, exact_dot(linv, work[here, :], ((1,), (0,))), 0.0)
        inv = exact_dot(linv, inverse[here, :], ((1,), (0,)))
        scaled = y * dinv
        work[...] = work[...] - exact_dot(scaled, y, ((0,), (0,)))
        inverse[...] = inverse[...] - exact_dot(scaled, inv, ((0,), (0,)))
        upper[here, :] = y
        upper[here, here] = unit
        inverse[here, :] = inv

    for copy in copies:
        copy.wait()
    g = dot3(split(inverse[...]), (turned[0], turned[1]), ((1,), (0,)))
    g_high[...], g_low[...] = split(g * w_ref[...])

    @pl.when(first_ref[0] == 1)
    def _():
        v_row = v_ref[...]
        lower = upper[...].T * (dinv_ref[...] / v_row)
        v_col = jnp.sum(jnp.where(one, v_row, 0.0), axis=1, keepdims=True)
        diag_ref[...] = v_col * jnp.where(col_id >= row_id, upper[...], lower)

    @pl.when(first_ref[0] == 0)
    def _():
        diag_ref[...] = jnp.zeros_like(diag_ref)


def factor_panel(first_rows, block, turned_high, turned_low, w, panel_v):
    shapes = [
        ((PANEL, PAIRS), BF16), ((PANEL, PAIRS), BF16), ((PANEL, PANEL), F32), ((1, PANEL), F32),
    ]
    square = VMEM((PANEL, PANEL), F32)
    small = VMEM((BLOCK, BLOCK), F32)

    def whole(shape):
        return pl.BlockSpec(shape, lambda i: (0, 0))

    return pl.pallas_call(
        panel_kernel,
        in_specs=[
            pl.BlockSpec(memory_space=pltpu.SMEM), whole((PANEL, PANEL)), IN_HBM, IN_HBM,
            whole((1, PAIRS)), whole((1, PANEL)),
        ],
        scratch_shapes=[
            VMEM((2, PANEL, PAIRS), BF16), pltpu.SemaphoreType.DMA((2,)),
            square, square, square, small, small,
        ],
        compiler_params=PARAMS,
        cost_estimate=cost(6),
        name="factor_panel",
        **whole_out(shapes),
    )(first_rows, block, turned_high, turned_low, w, panel_v)


def fetch(step, pieces, buffer, sems, count=1):
    def copies(s):
        for n in range(count):
            slot = (s % 2, n)
            yield pltpu.make_async_copy(pieces[s * count + n], buffer.at[slot], sems.at[slot])

    for s in range(len(pieces) // count):

        @pl.when(step == s)
        def _():
            if s == 0:
                for copy in copies(0):
                    copy.start()
            if (s + 1) * count < len(pieces):
                for copy in copies(s + 1):
                    copy.start()
            for copy in copies(s):
                copy.wait()

    return buffer.at[lax.rem(step, 2)]


def project_kernel(count, meta_ref, *refs):
    pairs, singles, refs = refs[: count - 1], refs[count - 1 : count + 1], refs[count + 1 :]
    pieces = [pair.at[n] for pair in pairs for n in range(2)] + list(singles)
    g_high, g_low, w_ref, dinv_ref, panel_v_ref, v_ref, diag_ref = refs[:7]
    t_high_ref, t_low_ref, left_ref, turned, buffer, sems = refs[-6:]
    step = pl.program_id(0)
    here = fetch(step, pieces, buffer, sems, 2)
    for n in range(2):
        half = meta_ref[count + n]

        @pl.loop(0, HALF // 256)
        def _(chunk):
            at = pl.multiple_of(chunk * 256, 256)
            to = pl.ds(pl.multiple_of(half * HALF + at, 256), 256)
            turned[0, :, to], turned[1, :, to] = split(here[n, pl.ds(at, 256), :].T)

    rows = (turned[0], turned[1])
    g = (g_high[...], g_low[...])
    left = dot3(rows, g, ((1,), (1,))) * dinv_ref[...]
    t = (rows[0].astype(F32) + rows[1].astype(F32)) * w_ref[...]
    t = (t - dot3(split(left), g, ((1,), (0,)))) * v_ref[...]
    t_high_ref[...], t_low_ref[...] = split(t)
    left_ref[...] = left * v_ref[...] / panel_v_ref[...]
    block = meta_ref[step]

    @pl.when((meta_ref[count + 2] == 1) & (block < PANEL // PIECE))
    def _():
        here = pl.ds(pl.multiple_of(block * PIECE, PIECE), PIECE)
        g = g_high[here, :].astype(F32) + g_low[here, :].astype(F32)
        t_high_ref[...], t_low_ref[...] = split(g * v_ref[...])
        left_ref[...] = diag_ref[here, :]


def project_rows(meta, pieces, g_high, g_low, w, dinv, panel_v, v, diag):
    count = len(pieces) - 1

    def fixed(shape):
        return pl.BlockSpec(shape, lambda i, m: (0, 0), pipeline_mode=pl.Buffered(1))

    def by_row(width):
        return pl.BlockSpec((PIECE, width), lambda i, m: (m[i], 0))

    return pl.pallas_call(
        functools.partial(project_kernel, count),
        out_shape=[
            jax.ShapeDtypeStruct((ROWS, PAIRS), BF16),
            jax.ShapeDtypeStruct((ROWS, PAIRS), BF16),
            jax.ShapeDtypeStruct((ROWS, PANEL), F32),
        ],
        grid_spec=pltpu.PrefetchScalarGridSpec(
            num_scalar_prefetch=1,
            grid=(count,),
            in_specs=[IN_HBM] * (count + 1)
            + [
                fixed((PANEL, PAIRS)), fixed((PANEL, PAIRS)), fixed((1, PAIRS)),
                fixed((1, PANEL)), fixed((1, PANEL)), by_row(1), fixed((PANEL, PANEL)),
            ],
            out_specs=[by_row(PAIRS), by_row(PAIRS), by_row(PANEL)],
            scratch_shapes=[
                VMEM((2, PIECE, PAIRS), BF16),
                VMEM((2, 2, HALF, PIECE), F32),
                pltpu.SemaphoreType.DMA((2, 2)),
            ],
        ),
        compiler_params=PARAMS,
        cost_estimate=cost(7 * count),
        name="project_rows",
    )(meta, *pieces, g_high, g_low, w, dinv, panel_v, v, diag)


def multiply_kernel(count, meta_ref, high_ref, low_ref, left_ref, *refs):
    pieces = refs[: 2 * count]
    out_ref, columns, buffer, sems = refs[-4:]
    step = pl.program_id(0)
    here = fetch(step, pieces, buffer, sems, 2)
    for n in range(2):
        at = pl.ds(pl.multiple_of(meta_ref[count + n] * HALF, HALF), HALF)
        columns[0, at, :], columns[1, at, :] = split(here[n])
    block = meta_ref[step]
    col_start, row_start = meta_ref[count + 2], meta_ref[count + 3]
    product = dot3((high_ref[...], low_ref[...]), (columns[0], columns[1]), ((1,), (0,)))
    row_id = lax.broadcasted_iota(jnp.int32, (ROWS, PIECE), 0)
    col_id = lax.broadcasted_iota(jnp.int32, (ROWS, PIECE), 1)
    shift = col_start + block * PIECE - row_start
    out_ref[...] = product + jnp.where(row_id - col_id == shift, 1.0, 0.0)

    @pl.when((col_start == 0) & (block < PANEL // PIECE))
    def _():
        start = pl.multiple_of(block * PIECE, PIECE)
        out_ref[...] = left_ref[:, pl.ds(start, PIECE)]


def multiply(meta, high, low, left, pieces):
    count = len(pieces) // 2

    def fixed(shape):
        return pl.BlockSpec(shape, lambda i, m: (0, 0), pipeline_mode=pl.Buffered(1))

    return pl.pallas_call(
        functools.partial(multiply_kernel, count),
        out_shape=jax.ShapeDtypeStruct((ROWS, COLS), F32),
        grid_spec=pltpu.PrefetchScalarGridSpec(
            num_scalar_prefetch=1,
            grid=(count,),
            in_specs=[fixed((ROWS, PAIRS)), fixed((ROWS, PAIRS)), fixed((ROWS, PANEL))]
            + [IN_HBM] * (2 * count),
            out_specs=pl.BlockSpec((ROWS, PIECE), lambda i, m: (0, m[i])),
            scratch_shapes=[
                VMEM((2, PAIRS, PIECE), BF16),
                VMEM((2, 2, HALF, PIECE), F32),
                pltpu.SemaphoreType.DMA((2, 2)),
            ],
        ),
        compiler_params=PARAMS,
        cost_estimate=cost(5 * count),
        name="multiply",
    )(meta, high, low, left, *pieces)


def table_lookup(positions, table):
    entries = table.shape[0]
    matches = positions[:, None] == jnp.arange(entries, dtype=jnp.int32)[None, :]
    return jnp.sum(jnp.where(matches, table[None, :], 0.0), axis=1)


def pair_weights(entries, valence_energy, conduction_energy):
    cond_count = conduction_energy.shape[0]
    gaps = table_lookup(entries % cond_count, conduction_energy) - table_lookup(
        entries // cond_count, valence_energy
    )
    return 4.0 / gaps


def shards(piece, pair_list, valence_energy, conduction_energy, coulomb):
    x, k, h, z, l = [lax.axis_index(a) for a in AXES]
    first_rows = ((x == 0) & (k == 0) & (l == 0)).astype(jnp.int32)[None]

    own_w = pair_weights(pair_list, valence_energy, conduction_energy)
    own_small = jnp.concatenate([own_w, coulomb[:PANEL]])
    moved = move(own_small, other_band), move(piece, OUTER), move(piece, INNER)
    part, (far_small, outer, inner) = spread_panel(piece, moved, x, k, h, z, l)
    low, high = jnp.where(l == 0, own_small, far_small), jnp.where(l == 0, far_small, own_small)
    w = jnp.concatenate([low[:HALF], high[:HALF]])[None, :]
    extra = jnp.concatenate([low[None, HALF:], jnp.zeros((7, PANEL), F32)])
    part = jnp.concatenate([part, extra])
    ahead, back = move(part, x_ring(1)), move(part, x_ring(-1))
    parts = [part, ahead, back, move(ahead, x_ring(1))]
    parts += [move(p, other_core) for p in parts]
    first = jnp.where(h == l, inner, outer)
    second = jnp.where(h == l, piece, move(outer, RELAY))
    pair = jnp.stack([first, second])
    up, down = move(pair, z_ring(1)), move(pair, z_ring(-1))

    sign = 1 - 2 * k
    at = jnp.stack([x, x - sign, x + sign, x + 2, x, x + sign, x - sign, x + 2]) & 3
    core = jnp.stack([k] * 4 + [1 - k] * 4)
    slot = core * 4 + at
    from_first = jnp.sum(jnp.where(slot == 0, jnp.arange(8), 0), keepdims=True)
    panel_meta = jnp.concatenate([slot, from_first]).astype(jnp.int32)

    parts, columns = lax.optimization_barrier((parts, piece))
    own = move(columns, to_column_line)
    panel_high, panel_low, block, panel_v = prepare_panel(panel_meta, w, parts)
    g_high, g_low, diag, dinv = factor_panel(first_rows, block, panel_high, panel_low, w, panel_v)

    dinv, up, down = lax.optimization_barrier((dinv, up, down))
    row_pieces = [pair, up, down, move(up[0], z_ring(1)), move(down[1], z_ring(-1))]
    dinv, own = lax.optimization_barrier((dinv, own))
    far = move(own, other_band)
    own_ahead, own_back = move(own, x_ring(1)), move(own, x_ring(-1))

    far_ahead, far_back = move(far, x_ring(1)), move(far, x_ring(-1))
    own_across = move(own_ahead, x_ring(1))
    row_blocks = [z, (z + 3) & 3, (z + 1) & 3, (z + 2) & 3]
    rows_meta = jnp.stack(row_blocks + [1 - l, l, first_rows[0]]).astype(jnp.int32)
    t_high, t_low, left = project_rows(
        rows_meta, row_pieces, g_high, g_low, w, dinv, panel_v, coulomb[:, None], diag
    )

    t_high, far_ahead, far_back, own_across = lax.optimization_barrier(
        (t_high, far_ahead, far_back, own_across)
    )
    pieces = [own, far, own_ahead, far_ahead, own_back, far_back]
    pieces += [own_across, move(far_ahead, x_ring(1))]
    pieces += [move(p, other_core) for p in pieces]

    offset = (at - (2 * h + (z >> 1))) & 3
    blocks = 4 * core + 2 * (offset & 1) + (offset >> 1)
    tail = jnp.stack([l, 1 - l, (4 * h + z) * COLS, ((2 * x + k) * 2 + l) * ROWS])

    meta = jnp.concatenate([blocks, tail]).astype(jnp.int32)
    return multiply(meta, t_high, t_low, left, pieces)


def solution(mesh):
    fine = Mesh(mesh.devices.reshape(SIZES), AXES)
    in_specs = (P("l", ("x", "k", "h", "z")), P("l"), P(), P(), P(("x", "k", "l")))
    out_specs = P(("x", "k", "l"), ("h", "z"))
    return jax.shard_map(shards, mesh=fine, in_specs=in_specs, out_specs=out_specs, check_vma=False)
```

```python
import functools

import jax
import jax.numpy as jnp
from jax import lax
from jax.experimental import pallas as pl
from jax.experimental.pallas import tpu as pltpu
from jax.sharding import Mesh, PartitionSpec as P

PANEL = 512
PAIRS = 2048
HALF = 1024
ROWS = 1024
COLS = 2048
PIECE = 256
BLOCK = 128
PART = 128
GROUP = 8
AXES = ("x", "k", "h", "z", "l")
SIZES = (4, 2, 2, 4, 2)
F32 = jnp.float32
BF16 = jnp.bfloat16
VMEM = pltpu.VMEM
MIB = 2**20
PARAMS = pltpu.CompilerParams(vmem_limit_bytes=60 * MIB)
IN_HBM = pl.BlockSpec(memory_space=pltpu.HBM)


def cost(us):
    return pl.CostEstimate(flops=us * 10**9, bytes_accessed=us * 10**6, transcendentals=0)


def position(x, k, h, z, l):
    return (((x * 2 + k) * 2 + h) * 4 + z) * 2 + l


def move(value, target):
    pairs = []
    for x in range(4):
        for k in range(2):
            for h in range(2):
                for z in range(4):
                    for l in range(2):
                        to = target(x, k, h, z, l)
                        if to is not None:
                            pairs.append((position(x, k, h, z, l), position(*to)))
    return lax.ppermute(value, AXES, pairs)


def x_ring(step):
    return lambda x, k, h, z, l: ((x + (step if k == 0 else -step)) % 4, k, h, z, l)


def z_ring(step):
    return lambda x, k, h, z, l: (x, k, h, (z + step) % 4, l)


def other_core(x, k, h, z, l):
    return (x, 1 - k, h, z, l)


def other_band(x, k, h, z, l):
    return (x, k, h, z, 1 - l)


def to_column_line(x, k, h, z, l):
    return ((x + 2 * (z & 1) + (z >> 1)) % 4, h, x >> 1, (x & 1) * 2 + k, l)


def along_y(table):
    def target(x, k, h, z, l):
        to = table.get(2 * h + l)
        return None if to is None else (x, k, to >> 1, z, to & 1)

    return target


OUTER = along_y({0: 3, 3: 0, 1: 2, 2: 1})
INNER = along_y({1: 0, 2: 3})
RELAY = along_y({3: 2, 0: 1})


def spread_panel(piece, others, x, k, h, z, l):
    def source(h, z):
        return h == 0 and z < 2

    part = move(
        piece[512:], lambda x, k, h, z, l: (0, 1, 0, z, l) if x == k == 0 and source(h, z) else None
    )
    held = jnp.where(k == 1, part, piece[:512])
    part = move(held[256:], lambda x, k, h, z, l: (2, k, 0, z, l) if x == 0 and source(h, z) else None)
    held = jnp.where(x >= 2, part, held[:256])
    part = move(
        held[128:],
        lambda x, k, h, z, l: (x + 1, k, 0, z, l) if x % 2 == 0 and source(h, z) else None,
    )
    held = jnp.where(x % 2 == 1, part, held[:128])
    held, others = lax.optimization_barrier((held, others))
    part = move(held, lambda x, k, h, z, l: (x, k, h, z, 1 - l) if source(h, z) else None)
    low = l == 0
    held = jnp.stack([jnp.where(low, held, part), jnp.where(low, part, held)])
    part = move(held, lambda x, k, h, z, l: (x, k, 1, z, l) if source(h, z) else None)
    held = jnp.where(h == 1, part, held)
    held, others = lax.optimization_barrier((held, others))
    part = move(held, lambda x, k, h, z, l: (x, k, h, z + 2, l) if z < 2 else None)
    held = jnp.where(z >= 2, part, held)
    part = move(held, lambda x, k, h, z, l: (x, k, h, z ^ 1, l))
    even = z % 2 == 0
    both = jnp.concatenate([jnp.where(even, held, part), jnp.where(even, part, held)], axis=2)
    return both.reshape(2 * PART, PANEL), others


def split3(value):
    high = value.astype(BF16)
    rest = value - high.astype(F32)
    middle = rest.astype(BF16)
    return high, middle, (rest - middle.astype(F32)).astype(BF16)


def exact_dot(a, b, dims):
    a, b = split3(a), split3(b)
    left = jnp.concatenate([a[2], a[0], a[1], a[1], a[0], a[0]], axis=dims[0][0])
    right = jnp.concatenate([b[0], b[2], b[1], b[0], b[1], b[0]], axis=dims[1][0])
    return lax.dot_general(left, right, (dims, ((), ())), preferred_element_type=F32)


def factor_unit(a):
    n = BLOCK
    row_id = lax.broadcasted_iota(jnp.int32, (n, n), 0)
    col_id = lax.broadcasted_iota(jnp.int32, (n, n), 1)
    inv = jnp.where(row_id == col_id, 1.0, 0.0).astype(F32)
    upper_rows, inverse_rows = [], []
    for first in range(0, n, GROUP):
        m = n - first
        cols = [jnp.broadcast_to(a[:, first + t : first + t + 1], (m, n)) for t in range(GROUP)]
        rows = [a[t : t + 1, :] for t in range(GROUP)]
        irows = [inv[t : t + 1, :] for t in range(GROUP)]
        below = lax.broadcasted_iota(jnp.int32, (m, n), 0) >= GROUP
        for t in range(GROUP):
            recip = 1.0 / cols[t][t : t + 1, :]
            for u in range(t + 1, GROUP):
                factor = cols[t][u : u + 1, :] * recip
                rows[u] = rows[u] - factor * rows[t]
                irows[u] = irows[u] - factor * irows[t]
                cols[u] = cols[u] - cols[t] * factor
            low = jnp.where(below, cols[t], 0.0)
            a = a - low * (rows[t] * recip)
            inv = inv - low * (irows[t] * recip)
            upper_rows.append(rows[t])
            inverse_rows.append(irows[t])
        if m > GROUP:
            a, inv = a[GROUP:, :], inv[GROUP:, :]
    return upper_rows, inverse_rows


def split(value):
    high = value.astype(BF16)
    return high, (value - high.astype(F32)).astype(BF16)


def dot3(a, b, dims):
    left = jnp.concatenate([a[0], a[1], a[0]], axis=dims[0][0])
    right = jnp.concatenate([b[0], b[0], b[1]], axis=dims[1][0])
    return lax.dot_general(left, right, (dims, ((), ())), preferred_element_type=F32)


def prepare_kernel(meta_ref, w_ref, *refs):
    parts, refs = refs[:8], refs[8:]
    turned_high, turned_low, block_ref, v_ref, left, right, chunk, sems = refs
    n = PANEL
    copies = [
        pltpu.make_async_copy(part, chunk.at[s], sems.at[s]) for s, part in enumerate(parts)
    ]
    for copy in copies:
        copy.start()
    for s, copy in enumerate(copies):
        copy.wait()
        for half in range(2):
            at = pl.ds(pl.multiple_of(half * HALF + meta_ref[s] * PART, PART), PART)
            rows = chunk[s, half * PART : (half + 1) * PART, :]
            turn = rows.T
            turned_high[:, at], turned_low[:, at] = split(turn)
            left[0, :, at], left[1, :, at] = split(turn * w_ref[:, at])
            right[0, at, :], right[1, at, :] = split(rows)

    v_ref[...] = chunk[meta_ref[8], 2 * PART : 2 * PART + 1, :]
    row_id = lax.broadcasted_iota(jnp.int32, (n, n), 0)
    col_id = lax.broadcasted_iota(jnp.int32, (n, n), 1)
    block_ref[...] = jnp.where(row_id == col_id, 1.0 / v_ref[...], 0.0) + dot3(
        (left[0], left[1]), (right[0], right[1]), ((1,), (0,))
    )


def whole_out(shapes):
    return dict(
        out_shape=[jax.ShapeDtypeStruct(*shape) for shape in shapes],
        out_specs=[pl.BlockSpec(shape, lambda i: (0, 0)) for shape, _ in shapes],
        grid=(1,),
    )


def prepare_panel(meta, w, parts):
    shapes = [
        ((PANEL, PAIRS), BF16), ((PANEL, PAIRS), BF16), ((PANEL, PANEL), F32), ((1, PANEL), F32),
    ]
    return pl.pallas_call(
        prepare_kernel,
        in_specs=[
            pl.BlockSpec(memory_space=pltpu.SMEM), pl.BlockSpec((1, PAIRS), lambda i: (0, 0))
        ] + [IN_HBM] * 8,
        scratch_shapes=[
            VMEM((2, PANEL, PAIRS), BF16), VMEM((2, PAIRS, PANEL), BF16),
            VMEM((8, *parts[0].shape), F32), pltpu.SemaphoreType.DMA((8,)),
        ],
        compiler_params=PARAMS,
        cost_estimate=cost(2),
        name="prepare_panel",
        **whole_out(shapes),
    )(meta, w, *parts)


def panel_kernel(
    first_ref, block_ref, turned_high, turned_low, w_ref, v_ref, g_high, g_low, diag_ref, dinv_ref,
    turned, sems, work, upper, inverse, ywork, iwork,
):
    n = PANEL
    copies = [
        pltpu.make_async_copy(ref, turned.at[i], sems.at[i])
        for i, ref in enumerate((turned_high, turned_low))
    ]
    for copy in copies:
        copy.start()
    row_id = lax.broadcasted_iota(jnp.int32, (n, n), 0)
    col_id = lax.broadcasted_iota(jnp.int32, (n, n), 1)
    one = row_id == col_id
    work[...] = block_ref[...]
    inverse[...] = jnp.where(one, 1.0, 0.0).astype(F32)
    br = lax.broadcasted_iota(jnp.int32, (BLOCK, BLOCK), 0)
    bc = lax.broadcasted_iota(jnp.int32, (BLOCK, BLOCK), 1)
    wide = lax.broadcasted_iota(jnp.int32, (BLOCK, n), 1)

    @pl.loop(0, n // BLOCK)
    def _(step):
        s = pl.multiple_of(step * BLOCK, BLOCK)
        here = pl.ds(s, BLOCK)
        upper_rows, inverse_rows = factor_unit(work[here, here])
        for j in range(BLOCK):
            ywork[j : j + 1, :] = upper_rows[j]
            iwork[j : j + 1, :] = inverse_rows[j]
        unit = jnp.where(bc >= br, ywork[...], 0.0)
        linv = iwork[...]
        diag = jnp.where(bc == br, unit, 0.0)
        dinv = 1.0 / jnp.sum(diag, axis=1, keepdims=True)
        dinv_ref[:, here] = 1.0 / jnp.sum(diag, axis=0, keepdims=True)
        y = jnp.where(wide >= s + BLOCK, exact_dot(linv, work[here, :], ((1,), (0,))), 0.0)
        inv = exact_dot(linv, inverse[here, :], ((1,), (0,)))
        scaled = y * dinv
        work[...] = work[...] - exact_dot(scaled, y, ((0,), (0,)))
        inverse[...] = inverse[...] - exact_dot(scaled, inv, ((0,), (0,)))
        upper[here, :] = y
        upper[here, here] = unit
        inverse[here, :] = inv

    for copy in copies:
        copy.wait()
    g = dot3(split(inverse[...]), (turned[0], turned[1]), ((1,), (0,)))
    g_high[...], g_low[...] = split(g * w_ref[...])

    @pl.when(first_ref[0] == 1)
    def _():
        v_row = v_ref[...]
        lower = upper[...].T * (dinv_ref[...] / v_row)
        v_col = jnp.sum(jnp.where(one, v_row, 0.0), axis=1, keepdims=True)
        diag_ref[...] = v_col * jnp.where(col_id >= row_id, upper[...], lower)

    @pl.when(first_ref[0] == 0)
    def _():
        diag_ref[...] = jnp.zeros_like(diag_ref)


def factor_panel(first_rows, block, turned_high, turned_low, w, panel_v):
    shapes = [
        ((PANEL, PAIRS), BF16), ((PANEL, PAIRS), BF16), ((PANEL, PANEL), F32), ((1, PANEL), F32),
    ]
    square = VMEM((PANEL, PANEL), F32)
    small = VMEM((BLOCK, BLOCK), F32)

    def whole(shape):
        return pl.BlockSpec(shape, lambda i: (0, 0))

    return pl.pallas_call(
        panel_kernel,
        in_specs=[
            pl.BlockSpec(memory_space=pltpu.SMEM), whole((PANEL, PANEL)), IN_HBM, IN_HBM,
            whole((1, PAIRS)), whole((1, PANEL)),
        ],
        scratch_shapes=[
            VMEM((2, PANEL, PAIRS), BF16), pltpu.SemaphoreType.DMA((2,)),
            square, square, square, small, small,
        ],
        compiler_params=PARAMS,
        cost_estimate=cost(6),
        name="factor_panel",
        **whole_out(shapes),
    )(first_rows, block, turned_high, turned_low, w, panel_v)


def fetch(step, pieces, buffer, sems, count=1):
    def copies(s):
        for n in range(count):
            slot = (s % 2, n)
            yield pltpu.make_async_copy(pieces[s * count + n], buffer.at[slot], sems.at[slot])

    for s in range(len(pieces) // count):

        @pl.when(step == s)
        def _():
            if s == 0:
                for copy in copies(0):
                    copy.start()
            if (s + 1) * count < len(pieces):
                for copy in copies(s + 1):
                    copy.start()
            for copy in copies(s):
                copy.wait()

    return buffer.at[lax.rem(step, 2)]


def project_kernel(count, meta_ref, *refs):
    pairs, singles, refs = refs[: count - 1], refs[count - 1 : count + 1], refs[count + 1 :]
    pieces = [pair.at[n] for pair in pairs for n in range(2)] + list(singles)
    g_high, g_low, w_ref, dinv_ref, panel_v_ref, v_ref, diag_ref = refs[:7]
    t_high_ref, t_low_ref, left_ref, turned, buffer, sems = refs[-6:]
    step = pl.program_id(0)
    here = fetch(step, pieces, buffer, sems, 2)
    for n in range(2):
        half = meta_ref[count + n]

        @pl.loop(0, HALF // 256)
        def _(chunk):
            at = pl.multiple_of(chunk * 256, 256)
            to = pl.ds(pl.multiple_of(half * HALF + at, 256), 256)
            turned[0, :, to], turned[1, :, to] = split(here[n, pl.ds(at, 256), :].T)

    rows = (turned[0], turned[1])
    g = (g_high[...], g_low[...])
    left = dot3(rows, g, ((1,), (1,))) * dinv_ref[...]
    t = (rows[0].astype(F32) + rows[1].astype(F32)) * w_ref[...]
    t = (t - dot3(split(left), g, ((1,), (0,)))) * v_ref[...]
    t_high_ref[...], t_low_ref[...] = split(t)
    left_ref[...] = left * v_ref[...] / panel_v_ref[...]
    block = meta_ref[step]

    @pl.when((meta_ref[count + 2] == 1) & (block < PANEL // PIECE))
    def _():
        here = pl.ds(pl.multiple_of(block * PIECE, PIECE), PIECE)
        g = g_high[here, :].astype(F32) + g_low[here, :].astype(F32)
        t_high_ref[...], t_low_ref[...] = split(g * v_ref[...])
        left_ref[...] = diag_ref[here, :]


def project_rows(meta, pieces, g_high, g_low, w, dinv, panel_v, v, diag):
    count = len(pieces) - 1

    def fixed(shape):
        return pl.BlockSpec(shape, lambda i, m: (0, 0), pipeline_mode=pl.Buffered(1))

    def by_row(width):
        return pl.BlockSpec((PIECE, width), lambda i, m: (m[i], 0))

    return pl.pallas_call(
        functools.partial(project_kernel, count),
        out_shape=[
            jax.ShapeDtypeStruct((ROWS, PAIRS), BF16),
            jax.ShapeDtypeStruct((ROWS, PAIRS), BF16),
            jax.ShapeDtypeStruct((ROWS, PANEL), F32),
        ],
        grid_spec=pltpu.PrefetchScalarGridSpec(
            num_scalar_prefetch=1,
            grid=(count,),
            in_specs=[IN_HBM] * (count + 1)
            + [
                fixed((PANEL, PAIRS)), fixed((PANEL, PAIRS)), fixed((1, PAIRS)),
                fixed((1, PANEL)), fixed((1, PANEL)), by_row(1), fixed((PANEL, PANEL)),
            ],
            out_specs=[by_row(PAIRS), by_row(PAIRS), by_row(PANEL)],
            scratch_shapes=[
                VMEM((2, PIECE, PAIRS), BF16),
                VMEM((2, 2, HALF, PIECE), F32),
                pltpu.SemaphoreType.DMA((2, 2)),
            ],
        ),
        compiler_params=PARAMS,
        cost_estimate=cost(7 * count),
        name="project_rows",
    )(meta, *pieces, g_high, g_low, w, dinv, panel_v, v, diag)


def multiply_kernel(last, meta_ref, high_ref, low_ref, *refs):
    pieces, refs = refs[:8], refs[8:]
    out_ref, buffer, sems = refs[-3:]
    step = pl.program_id(0)
    piece = fetch(step, pieces, buffer, sems)
    product = dot3((high_ref[...], low_ref[...]), split(piece[0]), ((1,), (0,)))
    if not last:
        out_ref[...] = product
    else:
        total_ref, left_ref = refs[:2]
        block = meta_ref[step]
        row_id = lax.broadcasted_iota(jnp.int32, (ROWS, PIECE), 0)
        col_id = lax.broadcasted_iota(jnp.int32, (ROWS, PIECE), 1)
        shift = meta_ref[9] + block * PIECE - meta_ref[10]
        one = jnp.where(row_id - col_id == shift, 1.0, 0.0)
        out_ref[...] = total_ref[...] + product + one

        @pl.when((meta_ref[9] == 0) & (block < PANEL // PIECE))
        def _():
            start = pl.multiple_of(block * PIECE, PIECE)
            out_ref[...] = left_ref[:, pl.ds(start, PIECE)]


def multiply(meta, high, low, pieces, total=None, left=None):
    last = total is not None
    halves = pl.BlockSpec((ROWS, HALF), lambda i, m: (0, m[8]), pipeline_mode=pl.Buffered(1))
    column = pl.BlockSpec((ROWS, PIECE), lambda i, m: (0, m[i]))
    in_specs = [halves, halves] + [IN_HBM] * 8
    operands = [high, low, *pieces]
    aliases = {}
    if last:
        in_specs += [
            column,
            pl.BlockSpec((ROWS, PANEL), lambda i, m: (0, 0), pipeline_mode=pl.Buffered(1)),
        ]
        operands += [total, left]
        aliases = {11: 0}
    return pl.pallas_call(
        functools.partial(multiply_kernel, last),
        out_shape=jax.ShapeDtypeStruct((ROWS, COLS), F32),
        grid_spec=pltpu.PrefetchScalarGridSpec(
            num_scalar_prefetch=1,
            grid=(8,),
            in_specs=in_specs,
            out_specs=column,
            scratch_shapes=[VMEM((2, 1, HALF, PIECE), F32), pltpu.SemaphoreType.DMA((2, 1))],
        ),
        input_output_aliases=aliases,
        compiler_params=PARAMS,
        cost_estimate=cost(20),
        name="multiply_last" if last else "multiply_first",
    )(meta, *operands)


def table_lookup(positions, table):
    entries = table.shape[0]
    matches = positions[:, None] == jnp.arange(entries, dtype=jnp.int32)[None, :]
    return jnp.sum(jnp.where(matches, table[None, :], 0.0), axis=1)


def pair_weights(entries, valence_energy, conduction_energy):
    cond_count = conduction_energy.shape[0]
    gaps = table_lookup(entries % cond_count, conduction_energy) - table_lookup(
        entries // cond_count, valence_energy
    )
    return 4.0 / gaps


def shards(piece, pair_list, valence_energy, conduction_energy, coulomb):
    x, k, h, z, l = [lax.axis_index(a) for a in AXES]
    first_rows = ((x == 0) & (k == 0) & (l == 0)).astype(jnp.int32)[None]

    own_w = pair_weights(pair_list, valence_energy, conduction_energy)
    own_small = jnp.concatenate([own_w, coulomb[:PANEL]])
    moved = move(own_small, other_band), move(piece, OUTER), move(piece, INNER)
    part, (far_small, outer, inner) = spread_panel(piece, moved, x, k, h, z, l)
    low, high = jnp.where(l == 0, own_small, far_small), jnp.where(l == 0, far_small, own_small)
    w = jnp.concatenate([low[:HALF], high[:HALF]])[None, :]
    extra = jnp.concatenate([low[None, HALF:], jnp.zeros((7, PANEL), F32)])
    part = jnp.concatenate([part, extra])
    ahead, back = move(part, x_ring(1)), move(part, x_ring(-1))
    parts = [part, ahead, back, move(ahead, x_ring(1))]
    parts += [move(p, other_core) for p in parts]
    first = jnp.where(h == l, inner, outer)
    second = jnp.where(h == l, piece, move(outer, RELAY))
    pair = jnp.stack([first, second])
    up, down = move(pair, z_ring(1)), move(pair, z_ring(-1))

    sign = 1 - 2 * k
    at = jnp.stack([x, x - sign, x + sign, x + 2, x, x + sign, x - sign, x + 2]) & 3
    core = jnp.stack([k] * 4 + [1 - k] * 4)
    slot = core * 4 + at
    from_first = jnp.sum(jnp.where(slot == 0, jnp.arange(8), 0), keepdims=True)
    panel_meta = jnp.concatenate([slot, from_first]).astype(jnp.int32)

    parts, columns = lax.optimization_barrier((parts, piece))
    own = move(columns, to_column_line)
    panel_high, panel_low, block, panel_v = prepare_panel(panel_meta, w, parts)
    g_high, g_low, diag, dinv = factor_panel(first_rows, block, panel_high, panel_low, w, panel_v)

    dinv, up, down = lax.optimization_barrier((dinv, up, down))
    row_pieces = [pair, up, down, move(up[0], z_ring(1)), move(down[1], z_ring(-1))]
    dinv, own = lax.optimization_barrier((dinv, own))
    far = move(own, other_band)
    own_ahead, own_back = move(own, x_ring(1)), move(own, x_ring(-1))

    far_ahead, far_back = move(far, x_ring(1)), move(far, x_ring(-1))
    own_across = move(own_ahead, x_ring(1))
    row_blocks = [z, (z + 3) & 3, (z + 1) & 3, (z + 2) & 3]
    rows_meta = jnp.stack(row_blocks + [1 - l, l, first_rows[0]]).astype(jnp.int32)
    t_high, t_low, left = project_rows(
        rows_meta, row_pieces, g_high, g_low, w, dinv, panel_v, coulomb[:, None], diag
    )

    own_others = [move(p, other_core) for p in (own, own_ahead, own_back)]
    t_high, far_ahead, far_back, own_across = lax.optimization_barrier(
        (t_high, far_ahead, far_back, own_across)
    )
    far_across = move(far_ahead, x_ring(1))
    own_pieces = [own, own_ahead, own_back, own_across]
    own_pieces += own_others + [move(own_across, other_core)]
    far_others = [move(p, other_core) for p in (far, far_ahead, far_back)]

    offset = (at - (2 * h + (z >> 1))) & 3
    blocks = 4 * core + 2 * (offset & 1) + (offset >> 1)
    starts = [(4 * h + z) * COLS, ((2 * x + k) * 2 + l) * ROWS]

    def meta(half):
        return jnp.concatenate([blocks, jnp.stack([half] + starts)]).astype(jnp.int32)

    total = multiply(meta(l), t_high, t_low, own_pieces)
    total, far_across = lax.optimization_barrier((total, far_across))
    far_pieces = [far, far_ahead, far_back, far_across]
    far_pieces += far_others + [move(far_across, other_core)]
    return multiply(meta(1 - l), t_high, t_low, far_pieces, total, left)


def solution(mesh):
    fine = Mesh(mesh.devices.reshape(SIZES), AXES)
    in_specs = (P("l", ("x", "k", "h", "z")), P("l"), P(), P(), P(("x", "k", "l")))
    out_specs = P(("x", "k", "l"), ("h", "z"))
    return jax.shard_map(shards, mesh=fine, in_specs=in_specs, out_specs=out_specs, check_vma=False)
```

```python
import functools

import jax
import jax.numpy as jnp
from jax import lax
from jax.experimental import pallas as pl
from jax.experimental.pallas import tpu as pltpu
from jax.sharding import Mesh, PartitionSpec as P

PANEL = 512
PAIRS = 2048
HALF = 1024
ROWS = 1024
COLS = 2048
PIECE = 256
BLOCK = 128
PART = 128
GROUP = 8
AXES = ("x", "k", "h", "z", "l")
SIZES = (4, 2, 2, 4, 2)
F32 = jnp.float32
BF16 = jnp.bfloat16
VMEM = pltpu.VMEM
MIB = 2**20
PARAMS = pltpu.CompilerParams(vmem_limit_bytes=60 * MIB)
IN_HBM = pl.BlockSpec(memory_space=pltpu.HBM)


def cost(us):
    return pl.CostEstimate(flops=us * 10**9, bytes_accessed=us * 10**6, transcendentals=0)


def position(x, k, h, z, l):
    return (((x * 2 + k) * 2 + h) * 4 + z) * 2 + l


def move(value, target):
    pairs = []
    for x in range(4):
        for k in range(2):
            for h in range(2):
                for z in range(4):
                    for l in range(2):
                        to = target(x, k, h, z, l)
                        if to is not None:
                            pairs.append((position(x, k, h, z, l), position(*to)))
    return lax.ppermute(value, AXES, pairs)


def x_ring(step):
    return lambda x, k, h, z, l: ((x + (step if k == 0 else -step)) % 4, k, h, z, l)


def z_ring(step):
    return lambda x, k, h, z, l: (x, k, h, (z + step) % 4, l)


def other_core(x, k, h, z, l):
    return (x, 1 - k, h, z, l)


def other_band(x, k, h, z, l):
    return (x, k, h, z, 1 - l)


def to_column_line(x, k, h, z, l):
    return ((x + 2 * (z & 1) + (z >> 1)) % 4, h, x >> 1, (x & 1) * 2 + k, l)


def along_y(table):
    def target(x, k, h, z, l):
        to = table.get(2 * h + l)
        return None if to is None else (x, k, to >> 1, z, to & 1)

    return target


OUTER = along_y({0: 3, 3: 0, 1: 2, 2: 1})
INNER = along_y({1: 0, 2: 3})
RELAY = along_y({3: 2, 0: 1})


def spread_panel(piece, others, x, k, h, z, l):
    def source(h, z):
        return h == 0 and z < 2

    part = move(
        piece[512:], lambda x, k, h, z, l: (0, 1, 0, z, l) if x == k == 0 and source(h, z) else None
    )
    held = jnp.where(k == 1, part, piece[:512])
    part = move(held[256:], lambda x, k, h, z, l: (2, k, 0, z, l) if x == 0 and source(h, z) else None)
    held = jnp.where(x >= 2, part, held[:256])
    part = move(
        held[128:],
        lambda x, k, h, z, l: (x + 1, k, 0, z, l) if x % 2 == 0 and source(h, z) else None,
    )
    held = jnp.where(x % 2 == 1, part, held[:128])
    held, others = lax.optimization_barrier((held, others))
    part = move(held, lambda x, k, h, z, l: (x, k, h, z, 1 - l) if source(h, z) else None)
    low = l == 0
    held = jnp.stack([jnp.where(low, held, part), jnp.where(low, part, held)])
    part = move(held, lambda x, k, h, z, l: (x, k, 1, z, l) if source(h, z) else None)
    held = jnp.where(h == 1, part, held)
    held, others = lax.optimization_barrier((held, others))
    part = move(held, lambda x, k, h, z, l: (x, k, h, z + 2, l) if z < 2 else None)
    held = jnp.where(z >= 2, part, held)
    part = move(held, lambda x, k, h, z, l: (x, k, h, z ^ 1, l))
    even = z % 2 == 0
    both = jnp.concatenate([jnp.where(even, held, part), jnp.where(even, part, held)], axis=2)
    return both.reshape(2 * PART, PANEL), others


def split3(value):
    high = value.astype(BF16)
    rest = value - high.astype(F32)
    middle = rest.astype(BF16)
    return high, middle, (rest - middle.astype(F32)).astype(BF16)


def exact_dot(a, b, dims):
    a, b = split3(a), split3(b)
    left = jnp.concatenate([a[2], a[0], a[1], a[1], a[0], a[0]], axis=dims[0][0])
    right = jnp.concatenate([b[0], b[2], b[1], b[0], b[1], b[0]], axis=dims[1][0])
    return lax.dot_general(left, right, (dims, ((), ())), preferred_element_type=F32)


def factor_unit(a):
    n = BLOCK
    row_id = lax.broadcasted_iota(jnp.int32, (n, n), 0)
    col_id = lax.broadcasted_iota(jnp.int32, (n, n), 1)
    inv = jnp.where(row_id == col_id, 1.0, 0.0).astype(F32)
    upper_rows, inverse_rows = [], []
    for first in range(0, n, GROUP):
        m = n - first
        cols = [jnp.broadcast_to(a[:, first + t : first + t + 1], (m, n)) for t in range(GROUP)]
        rows = [a[t : t + 1, :] for t in range(GROUP)]
        irows = [inv[t : t + 1, :] for t in range(GROUP)]
        below = lax.broadcasted_iota(jnp.int32, (m, n), 0) >= GROUP
        for t in range(GROUP):
            recip = 1.0 / cols[t][t : t + 1, :]
            for u in range(t + 1, GROUP):
                factor = cols[t][u : u + 1, :] * recip
                rows[u] = rows[u] - factor * rows[t]
                irows[u] = irows[u] - factor * irows[t]
                cols[u] = cols[u] - cols[t] * factor
            low = jnp.where(below, cols[t], 0.0)
            a = a - low * (rows[t] * recip)
            inv = inv - low * (irows[t] * recip)
            upper_rows.append(rows[t])
            inverse_rows.append(irows[t])
        if m > GROUP:
            a, inv = a[GROUP:, :], inv[GROUP:, :]
    return upper_rows, inverse_rows


def split(value):
    high = value.astype(BF16)
    return high, (value - high.astype(F32)).astype(BF16)


def dot3(a, b, dims):
    left = jnp.concatenate([a[0], a[1], a[0]], axis=dims[0][0])
    right = jnp.concatenate([b[0], b[0], b[1]], axis=dims[1][0])
    return lax.dot_general(left, right, (dims, ((), ())), preferred_element_type=F32)


def prepare_kernel(meta_ref, w_ref, *refs):
    parts, refs = refs[:8], refs[8:]
    turned_high, turned_low, block_ref, v_ref, left, right, chunk, sems = refs
    n = PANEL
    copies = [
        pltpu.make_async_copy(part, chunk.at[s], sems.at[s]) for s, part in enumerate(parts)
    ]
    for copy in copies:
        copy.start()
    for s, copy in enumerate(copies):
        copy.wait()
        for half in range(2):
            at = pl.ds(pl.multiple_of(half * HALF + meta_ref[s] * PART, PART), PART)
            rows = chunk[s, half * PART : (half + 1) * PART, :]
            turn = rows.T
            turned_high[:, at], turned_low[:, at] = split(turn)
            left[0, :, at], left[1, :, at] = split(turn * w_ref[:, at])
            right[0, at, :], right[1, at, :] = split(rows)

    v_ref[...] = chunk[meta_ref[8], 2 * PART : 2 * PART + 1, :]
    row_id = lax.broadcasted_iota(jnp.int32, (n, n), 0)
    col_id = lax.broadcasted_iota(jnp.int32, (n, n), 1)
    block_ref[...] = jnp.where(row_id == col_id, 1.0 / v_ref[...], 0.0) + dot3(
        (left[0], left[1]), (right[0], right[1]), ((1,), (0,))
    )


def whole_out(shapes):
    return dict(
        out_shape=[jax.ShapeDtypeStruct(*shape) for shape in shapes],
        out_specs=[pl.BlockSpec(shape, lambda i: (0, 0)) for shape, _ in shapes],
        grid=(1,),
    )


def prepare_panel(meta, w, parts):
    shapes = [
        ((PANEL, PAIRS), BF16), ((PANEL, PAIRS), BF16), ((PANEL, PANEL), F32), ((1, PANEL), F32),
    ]
    return pl.pallas_call(
        prepare_kernel,
        in_specs=[
            pl.BlockSpec(memory_space=pltpu.SMEM), pl.BlockSpec((1, PAIRS), lambda i: (0, 0))
        ] + [IN_HBM] * 8,
        scratch_shapes=[
            VMEM((2, PANEL, PAIRS), BF16), VMEM((2, PAIRS, PANEL), BF16),
            VMEM((8, *parts[0].shape), F32), pltpu.SemaphoreType.DMA((8,)),
        ],
        compiler_params=PARAMS,
        cost_estimate=cost(2),
        name="prepare_panel",
        **whole_out(shapes),
    )(meta, w, *parts)


def panel_kernel(
    first_ref, block_ref, turned_high, turned_low, w_ref, v_ref, g_high, g_low, diag_ref, dinv_ref,
    turned, sems, work, upper, inverse, ywork, iwork,
):
    n = PANEL
    copies = [
        pltpu.make_async_copy(ref, turned.at[i], sems.at[i])
        for i, ref in enumerate((turned_high, turned_low))
    ]
    for copy in copies:
        copy.start()
    row_id = lax.broadcasted_iota(jnp.int32, (n, n), 0)
    col_id = lax.broadcasted_iota(jnp.int32, (n, n), 1)
    one = row_id == col_id
    work[...] = block_ref[...]
    inverse[...] = jnp.where(one, 1.0, 0.0).astype(F32)
    br = lax.broadcasted_iota(jnp.int32, (BLOCK, BLOCK), 0)
    bc = lax.broadcasted_iota(jnp.int32, (BLOCK, BLOCK), 1)
    wide = lax.broadcasted_iota(jnp.int32, (BLOCK, n), 1)

    @pl.loop(0, n // BLOCK)
    def _(step):
        s = pl.multiple_of(step * BLOCK, BLOCK)
        here = pl.ds(s, BLOCK)
        upper_rows, inverse_rows = factor_unit(work[here, here])
        for j in range(BLOCK):
            ywork[j : j + 1, :] = upper_rows[j]
            iwork[j : j + 1, :] = inverse_rows[j]
        unit = jnp.where(bc >= br, ywork[...], 0.0)
        linv = iwork[...]
        diag = jnp.where(bc == br, unit, 0.0)
        dinv = 1.0 / jnp.sum(diag, axis=1, keepdims=True)
        dinv_ref[:, here] = 1.0 / jnp.sum(diag, axis=0, keepdims=True)
        y = jnp.where(wide >= s + BLOCK, exact_dot(linv, work[here, :], ((1,), (0,))), 0.0)
        inv = exact_dot(linv, inverse[here, :], ((1,), (0,)))
        scaled = y * dinv
        work[...] = work[...] - exact_dot(scaled, y, ((0,), (0,)))
        inverse[...] = inverse[...] - exact_dot(scaled, inv, ((0,), (0,)))
        upper[here, :] = y
        upper[here, here] = unit
        inverse[here, :] = inv

    for copy in copies:
        copy.wait()
    g = dot3(split(inverse[...]), (turned[0], turned[1]), ((1,), (0,)))
    g_high[...], g_low[...] = split(g * w_ref[...])

    @pl.when(first_ref[0] == 1)
    def _():
        v_row = v_ref[...]
        lower = upper[...].T * (dinv_ref[...] / v_row)
        v_col = jnp.sum(jnp.where(one, v_row, 0.0), axis=1, keepdims=True)
        diag_ref[...] = v_col * jnp.where(col_id >= row_id, upper[...], lower)

    @pl.when(first_ref[0] == 0)
    def _():
        diag_ref[...] = jnp.zeros_like(diag_ref)


def factor_panel(first_rows, block, turned_high, turned_low, w, panel_v):
    shapes = [
        ((PANEL, PAIRS), BF16), ((PANEL, PAIRS), BF16), ((PANEL, PANEL), F32), ((1, PANEL), F32),
    ]
    square = VMEM((PANEL, PANEL), F32)
    small = VMEM((BLOCK, BLOCK), F32)

    def whole(shape):
        return pl.BlockSpec(shape, lambda i: (0, 0))

    return pl.pallas_call(
        panel_kernel,
        in_specs=[
            pl.BlockSpec(memory_space=pltpu.SMEM), whole((PANEL, PANEL)), IN_HBM, IN_HBM,
            whole((1, PAIRS)), whole((1, PANEL)),
        ],
        scratch_shapes=[
            VMEM((2, PANEL, PAIRS), BF16), pltpu.SemaphoreType.DMA((2,)),
            square, square, square, small, small,
        ],
        compiler_params=PARAMS,
        cost_estimate=cost(6),
        name="factor_panel",
        **whole_out(shapes),
    )(first_rows, block, turned_high, turned_low, w, panel_v)


def fetch(step, pieces, buffer, sems, count=1):
    def copies(s):
        for n in range(count):
            slot = (s % 2, n)
            yield pltpu.make_async_copy(pieces[s * count + n], buffer.at[slot], sems.at[slot])

    for s in range(len(pieces) // count):

        @pl.when(step == s)
        def _():
            if s == 0:
                for copy in copies(0):
                    copy.start()
            if (s + 1) * count < len(pieces):
                for copy in copies(s + 1):
                    copy.start()
            for copy in copies(s):
                copy.wait()

    return buffer.at[lax.rem(step, 2)]


def project_kernel(count, meta_ref, *refs):
    pairs, singles, refs = refs[: count - 1], refs[count - 1 : count + 1], refs[count + 1 :]
    pieces = [pair.at[n] for pair in pairs for n in range(2)] + list(singles)
    g_high, g_low, w_ref, dinv_ref, panel_v_ref, v_ref, diag_ref = refs[:7]
    t_high_ref, t_low_ref, left_ref, turned, buffer, sems = refs[-6:]
    step = pl.program_id(0)
    here = fetch(step, pieces, buffer, sems, 2)
    for n in range(2):
        half = meta_ref[count + n]

        @pl.loop(0, HALF // 256)
        def _(chunk):
            at = pl.multiple_of(chunk * 256, 256)
            to = pl.ds(pl.multiple_of(half * HALF + at, 256), 256)
            turned[0, :, to], turned[1, :, to] = split(here[n, pl.ds(at, 256), :].T)

    rows = (turned[0], turned[1])
    g = (g_high[...], g_low[...])
    left = dot3(rows, g, ((1,), (1,))) * dinv_ref[...]
    t = (rows[0].astype(F32) + rows[1].astype(F32)) * w_ref[...]
    t = (t - dot3(split(left), g, ((1,), (0,)))) * v_ref[...]
    t_high_ref[...], t_low_ref[...] = split(t)
    left_ref[...] = left * v_ref[...] / panel_v_ref[...]
    block = meta_ref[step]

    @pl.when((meta_ref[count + 2] == 1) & (block < PANEL // PIECE))
    def _():
        here = pl.ds(pl.multiple_of(block * PIECE, PIECE), PIECE)
        g = g_high[here, :].astype(F32) + g_low[here, :].astype(F32)
        t_high_ref[...], t_low_ref[...] = split(g * v_ref[...])
        left_ref[...] = diag_ref[here, :]


def project_rows(meta, pieces, g_high, g_low, w, dinv, panel_v, v, diag):
    count = len(pieces) - 1

    def fixed(shape):
        return pl.BlockSpec(shape, lambda i, m: (0, 0), pipeline_mode=pl.Buffered(1))

    def by_row(width):
        return pl.BlockSpec((PIECE, width), lambda i, m: (m[i], 0))

    return pl.pallas_call(
        functools.partial(project_kernel, count),
        out_shape=[
            jax.ShapeDtypeStruct((ROWS, PAIRS), BF16),
            jax.ShapeDtypeStruct((ROWS, PAIRS), BF16),
            jax.ShapeDtypeStruct((ROWS, PANEL), F32),
        ],
        grid_spec=pltpu.PrefetchScalarGridSpec(
            num_scalar_prefetch=1,
            grid=(count,),
            in_specs=[IN_HBM] * (count + 1)
            + [
                fixed((PANEL, PAIRS)), fixed((PANEL, PAIRS)), fixed((1, PAIRS)),
                fixed((1, PANEL)), fixed((1, PANEL)), by_row(1), fixed((PANEL, PANEL)),
            ],
            out_specs=[by_row(PAIRS), by_row(PAIRS), by_row(PANEL)],
            scratch_shapes=[
                VMEM((2, PIECE, PAIRS), BF16),
                VMEM((2, 2, HALF, PIECE), F32),
                pltpu.SemaphoreType.DMA((2, 2)),
            ],
        ),
        compiler_params=PARAMS,
        cost_estimate=cost(7 * count),
        name="project_rows",
    )(meta, *pieces, g_high, g_low, w, dinv, panel_v, v, diag)


def multiply_kernel(last, meta_ref, high_ref, low_ref, *refs):
    pieces, refs = refs[:8], refs[8:]
    out_ref, buffer, sems = refs[-3:]
    step = pl.program_id(0)
    piece = fetch(step, pieces, buffer, sems)
    product = dot3((high_ref[...], low_ref[...]), split(piece[0]), ((1,), (0,)))
    if not last:
        out_ref[...] = product
    else:
        total_ref, left_ref = refs[:2]
        block = meta_ref[step]
        row_id = lax.broadcasted_iota(jnp.int32, (ROWS, PIECE), 0)
        col_id = lax.broadcasted_iota(jnp.int32, (ROWS, PIECE), 1)
        shift = meta_ref[9] + block * PIECE - meta_ref[10]
        one = jnp.where(row_id - col_id == shift, 1.0, 0.0)
        out_ref[...] = total_ref[...] + product + one

        @pl.when((meta_ref[9] == 0) & (block < PANEL // PIECE))
        def _():
            start = pl.multiple_of(block * PIECE, PIECE)
            out_ref[...] = left_ref[:, pl.ds(start, PIECE)]


def multiply(meta, high, low, pieces, total=None, left=None):
    last = total is not None
    halves = pl.BlockSpec((ROWS, HALF), lambda i, m: (0, m[8]), pipeline_mode=pl.Buffered(1))
    column = pl.BlockSpec((ROWS, PIECE), lambda i, m: (0, m[i]))
    in_specs = [halves, halves] + [IN_HBM] * 8
    operands = [high, low, *pieces]
    aliases = {}
    if last:
        in_specs += [
            column,
            pl.BlockSpec((ROWS, PANEL), lambda i, m: (0, 0), pipeline_mode=pl.Buffered(1)),
        ]
        operands += [total, left]
        aliases = {11: 0}
    return pl.pallas_call(
        functools.partial(multiply_kernel, last),
        out_shape=jax.ShapeDtypeStruct((ROWS, COLS), F32),
        grid_spec=pltpu.PrefetchScalarGridSpec(
            num_scalar_prefetch=1,
            grid=(8,),
            in_specs=in_specs,
            out_specs=column,
            scratch_shapes=[VMEM((2, 1, HALF, PIECE), F32), pltpu.SemaphoreType.DMA((2, 1))],
        ),
        input_output_aliases=aliases,
        compiler_params=PARAMS,
        cost_estimate=cost(20),
        name="multiply_last" if last else "multiply_first",
    )(meta, *operands)


def table_lookup(positions, table):
    entries = table.shape[0]
    matches = positions[:, None] == jnp.arange(entries, dtype=jnp.int32)[None, :]
    return jnp.sum(jnp.where(matches, table[None, :], 0.0), axis=1)


def pair_weights(entries, valence_energy, conduction_energy):
    cond_count = conduction_energy.shape[0]
    gaps = table_lookup(entries % cond_count, conduction_energy) - table_lookup(
        entries // cond_count, valence_energy
    )
    return 4.0 / gaps


def shards(piece, pair_list, valence_energy, conduction_energy, coulomb):
    x, k, h, z, l = [lax.axis_index(a) for a in AXES]
    first_rows = ((x == 0) & (k == 0) & (l == 0)).astype(jnp.int32)[None]

    own_w = pair_weights(pair_list, valence_energy, conduction_energy)
    own_small = jnp.concatenate([own_w, coulomb[:PANEL]])
    moved = move(own_small, other_band), move(piece, OUTER), move(piece, INNER)
    part, (far_small, outer, inner) = spread_panel(piece, moved, x, k, h, z, l)
    low, high = jnp.where(l == 0, own_small, far_small), jnp.where(l == 0, far_small, own_small)
    w = jnp.concatenate([low[:HALF], high[:HALF]])[None, :]
    extra = jnp.concatenate([low[None, HALF:], jnp.zeros((7, PANEL), F32)])
    part = jnp.concatenate([part, extra])
    ahead, back = move(part, x_ring(1)), move(part, x_ring(-1))
    ahead, back, columns = lax.optimization_barrier((ahead, back, piece))
    own = move(columns, to_column_line)
    parts = [part, ahead, back, move(ahead, x_ring(1))]
    parts += [move(p, other_core) for p in parts]
    first = jnp.where(h == l, inner, outer)
    second = jnp.where(h == l, piece, move(outer, RELAY))
    pair = jnp.stack([first, second])
    up, down = move(pair, z_ring(1)), move(pair, z_ring(-1))

    sign = 1 - 2 * k
    at = jnp.stack([x, x - sign, x + sign, x + 2, x, x + sign, x - sign, x + 2]) & 3
    core = jnp.stack([k] * 4 + [1 - k] * 4)
    slot = core * 4 + at
    from_first = jnp.sum(jnp.where(slot == 0, jnp.arange(8), 0), keepdims=True)
    panel_meta = jnp.concatenate([slot, from_first]).astype(jnp.int32)

    panel_high, panel_low, block, panel_v = prepare_panel(panel_meta, w, parts)
    g_high, g_low, diag, dinv = factor_panel(first_rows, block, panel_high, panel_low, w, panel_v)

    dinv, up, down = lax.optimization_barrier((dinv, up, down))
    row_pieces = [pair, up, down, move(up[0], z_ring(1)), move(down[1], z_ring(-1))]
    dinv, own = lax.optimization_barrier((dinv, own))
    far = move(own, other_band)
    own_ahead, own_back = move(own, x_ring(1)), move(own, x_ring(-1))

    far_ahead, far_back = move(far, x_ring(1)), move(far, x_ring(-1))
    own_across = move(own_ahead, x_ring(1))
    row_blocks = [z, (z + 3) & 3, (z + 1) & 3, (z + 2) & 3]
    rows_meta = jnp.stack(row_blocks + [1 - l, l, first_rows[0]]).astype(jnp.int32)
    t_high, t_low, left = project_rows(
        rows_meta, row_pieces, g_high, g_low, w, dinv, panel_v, coulomb[:, None], diag
    )

    own_others = [move(p, other_core) for p in (own, own_ahead, own_back)]
    t_high, far_ahead, far_back, own_across = lax.optimization_barrier(
        (t_high, far_ahead, far_back, own_across)
    )
    far_across = move(far_ahead, x_ring(1))
    own_pieces = [own, own_ahead, own_back, own_across]
    own_pieces += own_others + [move(own_across, other_core)]
    far_others = [move(p, other_core) for p in (far, far_ahead, far_back)]

    offset = (at - (2 * h + (z >> 1))) & 3
    blocks = 4 * core + 2 * (offset & 1) + (offset >> 1)
    starts = [(4 * h + z) * COLS, ((2 * x + k) * 2 + l) * ROWS]

    def meta(half):
        return jnp.concatenate([blocks, jnp.stack([half] + starts)]).astype(jnp.int32)

    total = multiply(meta(l), t_high, t_low, own_pieces)
    total, far_across = lax.optimization_barrier((total, far_across))
    far_pieces = [far, far_ahead, far_back, far_across]
    far_pieces += far_others + [move(far_across, other_core)]
    return multiply(meta(1 - l), t_high, t_low, far_pieces, total, left)


def solution(mesh):
    fine = Mesh(mesh.devices.reshape(SIZES), AXES)
    in_specs = (P("l", ("x", "k", "h", "z")), P("l"), P(), P(), P(("x", "k", "l")))
    out_specs = P(("x", "k", "l"), ("h", "z"))
    return jax.shard_map(shards, mesh=fine, in_specs=in_specs, out_specs=out_specs, check_vma=False)
```
